768 devices in a mesh: group: 24 (over z, x_lo), expert: 8 (over y), tensor: 4 (over x_hi, core).
Axes of the slice: x: 4 (x_hi: 2, x_lo: 2; x = x_hi * 2 + x_lo), y: 8, z: 12, core: 2. Of those that a mesh axis runs over, the one named last changes fastest.
Arguments:
- tokens: bfloat16 [4, 1536, 6144], P(None, ('group', 'expert')), may hold values from -6 to 6
- expert_ids: int32 [4, 1536, 2], P(None, ('group', 'expert')), may hold values from 0 to 7, all different within a row; in each aligned block of 8 rows (0 to 7, 8 to 15, ..., all dimensions but the last counted through in order) at most 4 rows name the same one
- gate_values: float32 [4, 1536, 2], P(None, ('group', 'expert')), may hold values from 0.2 to 1
- rollout_gate_up: bfloat16 [8, 2, 6144, 1024], P('expert', None, None, 'tensor'), may hold values from -0.078125 to 0.078125
- learner_gate_up: float32 [8, 2, 6144, 1024], P('expert', None, 'group', 'tensor'), may hold values from -0.688919 to 0.688919
- down_weight: bfloat16 [8, 1024, 6144], P('expert', 'tensor'), may hold values from -0.1875 to 0.1875
Outputs:
- mixed: bfloat16 [4, 1536, 6144], P(None, ('group', 'expert'), 'tensor')
The draws below stay inside these ranges and needn't reach their ends.
Inputs may be any that keep to these rules, and one draw needn't show every extreme that they name: `expert_ids`: in each step the 8 tokens of one device (aligned blocks of 8 rows) name one expert at most 4 times, and some block reaches 4; the 2 experts of a token differ.
All inputs are finite; a program needn't handle non-finite values.
Results may differ from the reference program's by a relative error of at most 0.014.
Values may be sent and summed in bfloat16 or wider, within the bound.
No kernel may reach another device: no remote copies, remote signals or barrier semaphores. Data moves between devices by JAX's collectives and lax.ppermute only.
A program may use at most 128 MiB of HBM per device.

```python
import math
import jax
import jax.numpy as jnp
import numpy as np
from jax import lax

D = 6144
FF = 1024
BLOCK = 128
TOP = 2
STEPS = 4
TOK_DEV = 8
EXPERTS = 8
CAP = 4
TOKENS = 1536
N_GROUP = 24
N_EXPERT = 8
N_TENSOR = 4


def draw_learner_gate_up(key, part):
    key = jax.random.fold_in(key, 11)
    row_key, col_key, value_key = jax.random.split(key, 3)
    log_low = math.log(0.3)
    log_high = math.log(3.0)
    row_scale = jnp.exp(jax.random.uniform(row_key, (EXPERTS, 2, D, 1), jnp.float32, log_low, log_high))
    col_scale = jnp.exp(jax.random.uniform(col_key, (EXPERTS, 2, 1, FF), jnp.float32, log_low, log_high))
    values = jnp.clip(jax.random.normal(value_key, (EXPERTS, 2, D, FF), jnp.float32), -6.0, 6.0)
    return values * row_scale * col_scale * D ** (-0.5)


def level_of(rng, extent, pieces, least, top_value):
    def one(dim, blocks):
        steps = jax.random.uniform(jax.random.fold_in(jax.random.fold_in(rng, 6), dim), (blocks,), jnp.float32, least / len(pieces), top_value / len(pieces))
        return jnp.repeat(jnp.exp(steps), extent[dim] // blocks).reshape((-1,) + (1,) * (len(extent) - dim - 1))

    level = one(*pieces[0])
    for cut in pieces[1:]:
        level = level * one(*cut)
    return level


def assign_block(key, own, number, rows, amount, top, bound, skew):
    order = jax.random.permutation(key, amount)
    heavy_load, ordinary = load_shares(amount, rows * top, bound, skew, True), load_shares(amount, rows * top, bound, skew, False)
    places = jnp.arange(amount)

    def named(tallies, rotation):
        used = int((tallies > 0).sum())
        fixed = max(1, used // 4)
        shifted = fixed + (places - fixed + rotation * (used - fixed)) % max(1, amount - fixed)
        return jnp.zeros((amount,), jnp.int32).at[order[jnp.where(places < fixed, places, shifted)]].set(jnp.asarray(tallies, jnp.int32))

    tallies = jnp.where(number % 4 == 0, named(heavy_load, number // 4), named(ordinary, number - number // 4 - 1))
    mixed = jax.random.permutation(jax.random.fold_in(own, 3), amount)
    source_of, taker = mixed[0:amount // 2 * 2:2], mixed[1:amount // 2 * 2:2]
    margin = jnp.minimum(tallies[source_of] - 1, bound - tallies[taker]) // 2
    margin = jnp.where((source_of == order[0]) | (taker == order[0]) | (tallies[taker] == 0), 0, jnp.maximum(margin, 0))
    shifted = jax.random.randint(jax.random.fold_in(own, 4), (amount // 2,), 0, 1 << 20) % (margin + 1)
    tallies = tallies.at[source_of].add(-shifted).at[taker].add(shifted)
    members = jnp.searchsorted(jnp.cumsum(tallies), jnp.arange(rows * top), side="right").astype(jnp.int32)
    listing = members.reshape(top, rows).T
    listing = listing[jax.random.permutation(jax.random.fold_in(own, 1), rows)]
    rotation = jax.random.randint(jax.random.fold_in(own, 2), (rows, 1), 0, top)
    return jnp.take_along_axis(listing, (jnp.arange(top)[None, :] + rotation) % top, axis=1)


def load_shares(count, total, bound, skew, full):
    loads = [(1 << 20) // math.isqrt(rank ** skew) + 1 for rank in range(1, count + 1)]
    largest = bound if full else min(bound, max(-(-total // count), total * loads[0] // sum(loads)))
    least = 1 if total - largest >= count - 1 else 0
    holding, spare = [largest] + [least] * (count - 1), total - largest - least * (count - 1)
    while spare > 0:
        candidates = [i for i in range(1, count) if holding[i] < largest] or [i for i in range(1, count) if holding[i] < bound]
        whole, remaining = sum([loads[i] for i in candidates]), spare
        for i in candidates:
            addition = min(bound - holding[i], max(1, remaining * loads[i] // whole), spare)
            holding[i] = holding[i] + addition
            spare = spare - addition
    return np.array(holding)


def gaussian(key, extent, spread, reach, cuts=(), dtype=jnp.bfloat16):
    factor_of = level_of(key, extent, cuts, -0.22, 0.18) if cuts else 1.0
    drawn = jax.random.normal(key, extent, jnp.float32) * spread * factor_of
    return jnp.minimum(jnp.maximum(drawn, -reach), reach).astype(dtype)


def setup_inputs(seed: int = 0) -> dict:
    key_list = jax.random.split(jax.random.key(seed), 7)
    tokens = gaussian(key_list[0], (STEPS, TOKENS, D), 1.0, 6.0, ((1, 192),))
    expert_ids_keys = jax.random.split(jax.random.fold_in(key_list[1], 1), STEPS * TOKENS // TOK_DEV)
    expert_ids_turns = jax.random.permutation(jax.random.fold_in(key_list[1], 3), STEPS * TOKENS // TOK_DEV)
    expert_ids = jax.vmap(lambda own, number: assign_block(jax.random.fold_in(key_list[1], 2), own, number, TOK_DEV, EXPERTS, TOP, CAP, 1))(expert_ids_keys, expert_ids_turns).reshape((STEPS, TOKENS, TOP))
    gate_values = jnp.clip(0.2 + 0.8 * jax.random.uniform(key_list[2], (STEPS, TOKENS, TOP), jnp.float32) ** level_of(key_list[2], (STEPS, TOKENS, TOP), ((1, 192),), -0.2, 0.2), 0.2, 1.0)
    rollout_gate_up = gaussian(key_list[3], (EXPERTS, 2, D, FF), D ** -0.5, 0.078125, ((0, 8), (3, 4)))
    learner_gate_up = draw_learner_gate_up(jax.random.fold_in(key_list[6], 71), 0)
    down_weight = gaussian(key_list[5], (EXPERTS, FF, D), FF ** -0.5, 0.1875, ((0, 8), (1, 4)))
    return {"tokens": tokens, "expert_ids": expert_ids, "gate_values": gate_values, "rollout_gate_up": rollout_gate_up, "learner_gate_up": learner_gate_up, "down_weight": down_weight}


clip_level = 2.0
epsilon = 1e-06

def block_scales(change):
    expert_count, pair_count, row_count, col_count = change.shape
    blocks = change.reshape(expert_count, pair_count, row_count // BLOCK, BLOCK, col_count // BLOCK, BLOCK)
    mean_square = lax.optimization_barrier(jnp.mean(blocks * blocks, axis=(3, 5)))
    return jnp.sqrt(mean_square + epsilon).astype(jnp.bfloat16)

def quantize(change, scales):
    expert_count, pair_count, row_count, col_count = change.shape
    blocks = change.reshape(expert_count, pair_count, row_count // BLOCK, BLOCK, col_count // BLOCK, BLOCK)
    expanded = scales.astype(jnp.float32)[:, :, :, None, :, None]
    levels = jnp.clip(blocks / expanded, -clip_level, clip_level)
    return levels.reshape(change.shape).astype(jnp.bfloat16)

def apply_levels(current, levels, per_row):
    expert_count, pair_count, row_count, col_count = current.shape
    expanded = levels.astype(jnp.float32).reshape(expert_count, pair_count, row_count, col_count // BLOCK, BLOCK)
    step_size = per_row.astype(jnp.float32)[..., None]
    added = (expanded * step_size).reshape(current.shape)
    return (current.astype(jnp.float32) + added).astype(jnp.bfloat16)

def reference(tokens, expert_ids, gate_values, rollout_gate_up, learner_gate_up, down_weight):
    change = learner_gate_up - rollout_gate_up.astype(jnp.float32)
    scales = block_scales(change)
    levels = quantize(change, scales)
    synced = apply_levels(rollout_gate_up, levels, jnp.repeat(scales, BLOCK, axis=2))
    quarter_units = FF // N_TENSOR
    most_rows = STEPS * N_GROUP * N_EXPERT * CAP
    flat_tokens = tokens.reshape(-1, D)
    flat_ids = expert_ids.reshape(-1, TOP)
    flat_gates = gate_values.reshape(-1, TOP)
    total = jnp.zeros(flat_tokens.shape, jnp.float32)
    for expert_index in range(EXPERTS):
        chosen = flat_ids == expert_index
        weight_of = lax.optimization_barrier(jnp.sum(jnp.where(chosen, flat_gates, jnp.zeros_like(flat_gates)), axis=1))
        used = jnp.any(chosen, axis=1).astype(jnp.int32)
        order = jnp.argsort(1 - used, stable=True)[:most_rows].astype(jnp.int32)
        rows_in = flat_tokens[order]
        gate = jnp.dot(rows_in, synced[expert_index, 0], preferred_element_type=jnp.float32)
        upper = jnp.dot(rows_in, synced[expert_index, 1], preferred_element_type=jnp.float32)
        hidden = (jax.nn.silu(gate) * upper).astype(jnp.bfloat16)
        summed = jnp.zeros((rows_in.shape[0], D), jnp.float32)
        for quarter in range(N_TENSOR):
            low_unit = quarter * quarter_units
            part = jnp.dot(hidden[:, low_unit:low_unit + quarter_units], down_weight[expert_index, low_unit:low_unit + quarter_units], preferred_element_type=jnp.float32).astype(jnp.bfloat16)
            summed = summed + lax.optimization_barrier(part).astype(jnp.float32)
        expert_out = lax.optimization_barrier(summed.astype(jnp.bfloat16)).astype(jnp.float32)
        total = total.at[order].add(weight_of[order][:, None] * expert_out)
    return total.astype(jnp.bfloat16).reshape(tokens.shape)
```

```python
import jax
import jax.numpy as jnp
from jax import lax
from jax.experimental import pallas as pl
from jax.experimental.pallas import tpu as pltpu
from jax.sharding import Mesh
from jax.sharding import PartitionSpec as P

BLOCK = 128
CAP = 4
STEP_SLOTS = 16
ORDER = (0, -1, 1, 2)
PARTS = 6
VMEM_BYTES = 48 * 1024 * 1024

clip_level = 2.0
epsilon = 1e-06


def sync_kernel(place, learner, rollout, out):
    core = place[0]
    units = learner.shape[3]
    for half in range(learner.shape[2] // BLOCK):
        rows = pl.ds(pl.multiple_of((half ^ core) * BLOCK, BLOCK), BLOCK)
        for matrix in range(2):
            for column in range(units // BLOCK):
                columns = pl.ds(column * BLOCK, BLOCK)
                current = rollout[0, matrix, rows, columns].astype(jnp.float32)
                change = learner[0, matrix, rows, columns] - current
                mean_square = jnp.sum(change * change, keepdims=True) * (1.0 / (BLOCK * BLOCK))
                scale = jnp.sqrt(mean_square + epsilon).astype(jnp.bfloat16).astype(jnp.float32)
                levels = jnp.clip(change / scale, -clip_level, clip_level)
                levels = levels.astype(jnp.bfloat16).astype(jnp.float32)
                out[half, :, pl.ds(matrix * units + column * BLOCK, BLOCK)] = (
                    current + levels * scale
                ).astype(jnp.bfloat16)


def slot_choice(first, second, experts, steps):
    rows = first.shape[0]
    per_step = rows // steps
    slots = experts * steps * CAP
    row = lax.broadcasted_iota(jnp.int32, (rows, slots), 0)
    slot = lax.broadcasted_iota(jnp.int32, (rows, slots), 1)
    expert = (slot // (steps * CAP)).astype(jnp.float32)
    from_first, from_second = first == expert, second == expert
    named = (from_first | from_second).astype(jnp.float32)
    later = lax.broadcasted_iota(jnp.int32, (rows, rows), 0)
    earlier = lax.broadcasted_iota(jnp.int32, (rows, rows), 1)
    before = (earlier < later) & (earlier // per_step == later // per_step)
    rank = jnp.dot(
        before.astype(jnp.bfloat16), named.astype(jnp.bfloat16), preferred_element_type=jnp.float32
    )
    here = (slot // CAP % steps == row // per_step) & (rank == (slot % CAP).astype(jnp.float32))
    return from_first & here, from_second & here


def pack_kernel(place, ids, gates, tokens, outgoing, combine):
    core, z_high = place[0], place[3]
    sign = 1 - 2 * core
    parts, rows, columns = outgoing.shape
    pieces = columns // BLOCK - 1
    steps = rows // 8
    experts = combine.shape[1] // (steps * CAP)
    first, second = ids[:, 0:1].astype(jnp.float32), ids[:, 1:2].astype(jnp.float32)
    chosen_first, chosen_second = slot_choice(first, second, experts, steps)
    combine[...] = jnp.where(chosen_first, gates[:, 0:1], 0.0) + jnp.where(
        chosen_second, gates[:, 1:2], 0.0
    )
    lane = lax.broadcasted_iota(jnp.int32, (rows, BLOCK), 1)
    tail = jnp.where(lane == 0, first, jnp.where(lane == 1, second, 0.0)).astype(jnp.bfloat16)
    for part in range(parts):
        for piece in range(pieces):
            owner = lax.rem(z_high + sign * ORDER[piece] + pieces, pieces)
            start = ((owner * parts + part) * 2 + core) * BLOCK
            outgoing[part, :, piece * BLOCK : (piece + 1) * BLOCK] = tokens[
                :, pl.ds(pl.multiple_of(start, BLOCK), BLOCK)
            ]
        outgoing[part, :, pieces * BLOCK :] = tail


def dispatch_kernel(arrived, outgoing):
    experts, parts, step_slots, columns = outgoing.shape
    steps = step_slots // CAP
    for part in range(parts):
        tail = arrived[part, :, columns:].astype(jnp.float32)
        chosen_first, chosen_second = slot_choice(tail[:, 0:1], tail[:, 1:2], experts, steps)
        select = (chosen_first | chosen_second).astype(jnp.float32).astype(jnp.bfloat16)
        moved = lax.dot_general(
            select,
            arrived[part, :, :columns],
            (((0,), (0,)), ((), ())),
            preferred_element_type=jnp.float32,
        ).astype(jnp.bfloat16)
        for expert in range(experts):
            outgoing[expert, part] = moved[expert * step_slots : (expert + 1) * step_slots]


def gate_up_kernel(own, other, here, first, second, far, out):
    total = None
    for piece, (across, weights) in enumerate(((0, here), (2, first), (1, second), (3, far))):
        rows = jnp.concatenate(
            [
                own[:, piece * BLOCK : (piece + 1) * BLOCK],
                other[:, across * BLOCK : (across + 1) * BLOCK],
            ],
            axis=1,
        )
        term = jnp.dot(
            rows,
            weights[...].reshape(2 * BLOCK, weights.shape[2]),
            preferred_element_type=jnp.float32,
        )
        total = term if total is None else total + term
    partial = total.astype(jnp.bfloat16)
    parts, slots, _ = out.shape
    experts = own.shape[0] // (parts * STEP_SLOTS)
    for expert in range(experts):
        for part in range(parts):
            at = (expert * parts + part) * STEP_SLOTS
            out[part, expert * STEP_SLOTS : (expert + 1) * STEP_SLOTS] = partial[
                at : at + STEP_SLOTS
            ]


def down_kernel(place, hidden, own, crossed, sibling, out):
    units = own.shape[1]
    tensor = place[1]
    total = None
    for flip, columns in enumerate((own[0], sibling[0], crossed[...], sibling[1])):
        at = pl.ds(pl.multiple_of((tensor ^ flip) * units, units), units)
        term = jnp.dot(hidden[:, at], columns, preferred_element_type=jnp.float32)
        total = term if total is None else total + term
    out[...] = total.astype(jnp.bfloat16)


def shards(tokens, expert_ids, gate_values, rollout_gate_up, learner_gate_up, down_weight):
    ring = lax.axis_size("z_hi")
    expert_count = lax.axis_size("expert")
    tensor_count = lax.axis_size(("x_hi", "core"))
    step_count, token_count, width = tokens.shape
    quarter = width // tensor_count
    own_rows, units = learner_gate_up.shape[2:]
    slots = expert_count * step_count * CAP
    tensor = lax.axis_index(("x_hi", "core"))
    group = lax.axis_index(("z_hi", "z_lo", "x_lo"))
    place = jnp.stack([tensor % 2, tensor, group, group // PARTS]).astype(jnp.int32)

    def whole(*shape):
        return pl.BlockSpec(shape, lambda i, p: (0,) * len(shape))

    def call(body, out_shape, in_specs, out_specs, name):
        return pl.pallas_call(
            body,
            grid_spec=pltpu.PrefetchScalarGridSpec(
                num_scalar_prefetch=1, grid=(1,), in_specs=in_specs, out_specs=out_specs
            ),
            out_shape=out_shape,
            compiler_params=pltpu.CompilerParams(vmem_limit_bytes=VMEM_BYTES),
            name=name,
        )

    flat_tokens = tokens.reshape(step_count * token_count, width)
    rows = step_count * token_count
    packed, combine = call(
        pack_kernel,
        [
            jax.ShapeDtypeStruct((PARTS, rows, (ring + 1) * BLOCK), jnp.bfloat16),
            jax.ShapeDtypeStruct((rows, slots), jnp.float32),
        ],
        [whole(rows, 2), whole(rows, 2), whole(rows, width)],
        [whole(PARTS, rows, (ring + 1) * BLOCK), whole(rows, slots)],
        "pack_rows",
    )(place, expert_ids.reshape(rows, 2), gate_values.reshape(rows, 2), flat_tokens)
    shared = lax.all_to_all(packed, ("z_lo", "x_lo"), split_axis=0, concat_axis=0, tiled=True)

    packed, learner_gate_up = lax.optimization_barrier((packed, learner_gate_up))
    synced = call(
        sync_kernel,
        jax.ShapeDtypeStruct((2, own_rows // 2, 2 * units), jnp.bfloat16),
        [
            whole(1, 2, own_rows, units),
            pl.BlockSpec((1, 2, own_rows, units), lambda i, p: (0, 0, p[2], 0)),
        ],
        whole(2, own_rows // 2, 2 * units),
        "sync_rows",
    )(place, learner_gate_up, rollout_gate_up)

    def along(value, sign):
        perm = [
            (i * 2 + core, (i + sign * (1 - 2 * core)) % ring * 2 + core)
            for i in range(ring)
            for core in range(2)
        ]
        return lax.ppermute(value, ("z_hi", "core"), perm)

    first = along(synced, 1)
    second = along(synced, -1)

    synced, shared = lax.optimization_barrier((synced, shared))
    outgoing = pl.pallas_call(
        dispatch_kernel,
        out_shape=jax.ShapeDtypeStruct(
            (expert_count, PARTS, step_count * CAP, ring * BLOCK), jnp.bfloat16
        ),
        compiler_params=pltpu.CompilerParams(vmem_limit_bytes=VMEM_BYTES),
        name="dispatch_rows",
    )(shared)
    outgoing, first = lax.optimization_barrier((outgoing, first))
    far = along(first, 1)
    arrived = lax.all_to_all(outgoing, "expert", split_axis=0, concat_axis=0, tiled=True)
    arrived, second, far = lax.optimization_barrier((arrived, second, far))
    own = arrived.reshape(PARTS * slots, ring * BLOCK)
    other = lax.ppermute(own, "core", [(0, 1), (1, 0)])

    crossed = lax.ppermute(
        lax.dynamic_slice_in_dim(down_weight[0], (1 - tensor // 2) * 2 * quarter, 2 * quarter, 1),
        ("x_lo", "x_hi", "core"),
        [(i, i ^ 6) for i in range(8)],
    )
    sibling = lax.ppermute(
        jnp.stack(
            [
                lax.dynamic_slice_in_dim(down_weight[0], (tensor ^ 1) * quarter, quarter, 1),
                lax.dynamic_slice_in_dim(crossed, (1 - tensor % 2) * quarter, quarter, 1),
            ]
        ),
        "core",
        [(0, 1), (1, 0)],
    )

    partial = pl.pallas_call(
        gate_up_kernel,
        out_shape=jax.ShapeDtypeStruct((PARTS, slots, 2 * units), jnp.bfloat16),
        compiler_params=pltpu.CompilerParams(vmem_limit_bytes=VMEM_BYTES),
        name="gate_up",
    )(own, other, synced, first, second, far)
    partial = lax.all_to_all(partial, ("z_lo", "x_lo"), split_axis=0, concat_axis=0, tiled=True)
    both = jnp.sum(partial.astype(jnp.float32), axis=0)
    hidden = (jax.nn.silu(both[:, :units]) * both[:, units:]).astype(jnp.bfloat16)
    hidden = lax.all_gather(hidden, ("x_hi", "core"), axis=1, tiled=True)
    expert_out = call(
        down_kernel,
        jax.ShapeDtypeStruct((slots, quarter), jnp.bfloat16),
        [
            whole(slots, tensor_count * units),
            pl.BlockSpec((1, units, quarter), lambda i, p: (0, 0, p[1])),
            pl.BlockSpec((units, quarter), lambda i, p: (0, p[0])),
            whole(2, units, quarter),
        ],
        whole(slots, quarter),
        "down",
    )(place, hidden, down_weight, crossed, sibling)
    back = lax.all_to_all(
        expert_out.reshape(expert_count, step_count * CAP, quarter),
        "expert",
        split_axis=0,
        concat_axis=0,
        tiled=True,
    )
    mixed = jnp.dot(
        combine,
        back.reshape(slots, quarter).astype(jnp.float32),
        precision=lax.Precision.HIGHEST,
    )
    return mixed.astype(jnp.bfloat16).reshape(step_count, token_count, quarter)


def solution(mesh):
    groups, experts, tensors = mesh.devices.shape
    split = Mesh(
        mesh.devices.reshape(groups // PARTS, PARTS // 2, 2, experts, tensors // 2, 2),
        ("z_hi", "z_lo", "x_lo", "expert", "x_hi", "core"),
    )
    group, tensor = ("z_hi", "z_lo", "x_lo"), ("x_hi", "core")
    in_specs = (
        P(None, (*group, "expert"), None),
        P(None, (*group, "expert"), None),
        P(None, (*group, "expert"), None),
        P("expert", None, None, tensor),
        P("expert", None, group, tensor),
        P("expert", tensor, None),
    )
    out_specs = P(None, (*group, "expert"), tensor)
    return jax.shard_map(shards, mesh=split, in_specs=in_specs, out_specs=out_specs, check_vma=False)
```

```python
import jax
import jax.numpy as jnp
from jax import lax
from jax.experimental import pallas as pl
from jax.experimental.pallas import tpu as pltpu
from jax.sharding import Mesh
from jax.sharding import PartitionSpec as P

BLOCK = 128
CAP = 4
STEP_SLOTS = 16
ORDER = (0, -1, 1, 2)
PARTS = 6
VMEM_BYTES = 48 * 1024 * 1024

clip_level = 2.0
epsilon = 1e-06


def sync_kernel(place, learner, rollout, out):
    core = place[0]
    units = learner.shape[3]
    for half in range(learner.shape[2] // BLOCK):
        rows = pl.ds(pl.multiple_of((half ^ core) * BLOCK, BLOCK), BLOCK)
        for matrix in range(2):
            for column in range(units // BLOCK):
                columns = pl.ds(column * BLOCK, BLOCK)
                current = rollout[0, matrix, rows, columns].astype(jnp.float32)
                change = learner[0, matrix, rows, columns] - current
                mean_square = jnp.sum(change * change, keepdims=True) * (1.0 / (BLOCK * BLOCK))
                scale = jnp.sqrt(mean_square + epsilon).astype(jnp.bfloat16).astype(jnp.float32)
                levels = jnp.clip(change / scale, -clip_level, clip_level)
                levels = levels.astype(jnp.bfloat16).astype(jnp.float32)
                out[half, :, pl.ds(matrix * units + column * BLOCK, BLOCK)] = (
                    current + levels * scale
                ).astype(jnp.bfloat16)


def slot_choice(first, second, experts, steps):
    rows = first.shape[0]
    per_step = rows // steps
    slots = experts * steps * CAP
    row = lax.broadcasted_iota(jnp.int32, (rows, slots), 0)
    slot = lax.broadcasted_iota(jnp.int32, (rows, slots), 1)
    expert = (slot // (steps * CAP)).astype(jnp.float32)
    from_first, from_second = first == expert, second == expert
    named = (from_first | from_second).astype(jnp.float32)
    later = lax.broadcasted_iota(jnp.int32, (rows, rows), 0)
    earlier = lax.broadcasted_iota(jnp.int32, (rows, rows), 1)
    before = (earlier < later) & (earlier // per_step == later // per_step)
    rank = jnp.dot(
        before.astype(jnp.bfloat16), named.astype(jnp.bfloat16), preferred_element_type=jnp.float32
    )
    here = (slot // CAP % steps == row // per_step) & (rank == (slot % CAP).astype(jnp.float32))
    return from_first & here, from_second & here


def pack_kernel(place, ids, gates, tokens, outgoing, combine):
    core, z_high = place[0], place[3]
    sign = 1 - 2 * core
    parts, rows, columns = outgoing.shape
    pieces = columns // BLOCK - 1
    steps = rows // 8
    experts = combine.shape[1] // (steps * CAP)
    first, second = ids[:, 0:1].astype(jnp.float32), ids[:, 1:2].astype(jnp.float32)
    chosen_first, chosen_second = slot_choice(first, second, experts, steps)
    combine[...] = jnp.where(chosen_first, gates[:, 0:1], 0.0) + jnp.where(
        chosen_second, gates[:, 1:2], 0.0
    )
    lane = lax.broadcasted_iota(jnp.int32, (rows, BLOCK), 1)
    tail = jnp.where(lane == 0, first, jnp.where(lane == 1, second, 0.0)).astype(jnp.bfloat16)
    for part in range(parts):
        for piece in range(pieces):
            owner = lax.rem(z_high + sign * ORDER[piece] + pieces, pieces)
            start = ((owner * parts + part) * 2 + core) * BLOCK
            outgoing[part, :, piece * BLOCK : (piece + 1) * BLOCK] = tokens[
                :, pl.ds(pl.multiple_of(start, BLOCK), BLOCK)
            ]
        outgoing[part, :, pieces * BLOCK :] = tail


def dispatch_kernel(arrived, outgoing):
    experts, parts, step_slots, columns = outgoing.shape
    steps = step_slots // CAP
    for part in range(parts):
        tail = arrived[part, :, columns:].astype(jnp.float32)
        chosen_first, chosen_second = slot_choice(tail[:, 0:1], tail[:, 1:2], experts, steps)
        select = (chosen_first | chosen_second).astype(jnp.float32).astype(jnp.bfloat16)
        moved = lax.dot_general(
            select,
            arrived[part, :, :columns],
            (((0,), (0,)), ((), ())),
            preferred_element_type=jnp.float32,
        ).astype(jnp.bfloat16)
        for expert in range(experts):
            outgoing[expert, part] = moved[expert * step_slots : (expert + 1) * step_slots]


def gate_up_kernel(own, other, here, first, second, far, out):
    total = None
    for piece, (across, weights) in enumerate(((0, here), (2, first), (1, second), (3, far))):
        rows = jnp.concatenate(
            [
                own[:, piece * BLOCK : (piece + 1) * BLOCK],
                other[:, across * BLOCK : (across + 1) * BLOCK],
            ],
            axis=1,
        )
        term = jnp.dot(
            rows,
            weights[...].reshape(2 * BLOCK, weights.shape[2]),
            preferred_element_type=jnp.float32,
        )
        total = term if total is None else total + term
    partial = total.astype(jnp.bfloat16)
    parts, slots, _ = out.shape
    experts = own.shape[0] // (parts * STEP_SLOTS)
    for expert in range(experts):
        for part in range(parts):
            at = (expert * parts + part) * STEP_SLOTS
            out[part, expert * STEP_SLOTS : (expert + 1) * STEP_SLOTS] = partial[
                at : at + STEP_SLOTS
            ]


def down_kernel(place, own, other, own_low, own_high, other_low, other_high, out):
    for side, (mine, theirs) in enumerate(((own_low, other_low), (own_high, other_high))):
        total = jnp.dot(own[...], mine[0], preferred_element_type=jnp.float32)
        total += jnp.dot(other[...], theirs[0], preferred_element_type=jnp.float32)
        out[side] = total.astype(jnp.bfloat16)


def shards(tokens, expert_ids, gate_values, rollout_gate_up, learner_gate_up, down_weight):
    ring = lax.axis_size("z_hi")
    expert_count = lax.axis_size("expert")
    tensor_count = lax.axis_size(("x_hi", "core"))
    step_count, token_count, width = tokens.shape
    quarter = width // tensor_count
    own_rows, units = learner_gate_up.shape[2:]
    slots = expert_count * step_count * CAP
    tensor = lax.axis_index(("x_hi", "core"))
    group = lax.axis_index(("z_hi", "z_lo", "x_lo"))
    place = jnp.stack([tensor % 2, tensor, group, group // PARTS]).astype(jnp.int32)

    def whole(*shape):
        return pl.BlockSpec(shape, lambda i, p: (0,) * len(shape))

    def call(body, out_shape, in_specs, out_specs, name):
        return pl.pallas_call(
            body,
            grid_spec=pltpu.PrefetchScalarGridSpec(
                num_scalar_prefetch=1, grid=(1,), in_specs=in_specs, out_specs=out_specs
            ),
            out_shape=out_shape,
            compiler_params=pltpu.CompilerParams(vmem_limit_bytes=VMEM_BYTES),
            name=name,
        )

    flat_tokens = tokens.reshape(step_count * token_count, width)
    rows = step_count * token_count
    packed, combine = call(
        pack_kernel,
        [
            jax.ShapeDtypeStruct((PARTS, rows, (ring + 1) * BLOCK), jnp.bfloat16),
            jax.ShapeDtypeStruct((rows, slots), jnp.float32),
        ],
        [whole(rows, 2), whole(rows, 2), whole(rows, width)],
        [whole(PARTS, rows, (ring + 1) * BLOCK), whole(rows, slots)],
        "pack_rows",
    )(place, expert_ids.reshape(rows, 2), gate_values.reshape(rows, 2), flat_tokens)
    shared = lax.all_to_all(packed, ("z_lo", "x_lo"), split_axis=0, concat_axis=0, tiled=True)

    packed, learner_gate_up = lax.optimization_barrier((packed, learner_gate_up))
    synced = call(
        sync_kernel,
        jax.ShapeDtypeStruct((2, own_rows // 2, 2 * units), jnp.bfloat16),
        [
            whole(1, 2, own_rows, units),
            pl.BlockSpec((1, 2, own_rows, units), lambda i, p: (0, 0, p[2], 0)),
        ],
        whole(2, own_rows // 2, 2 * units),
        "sync_rows",
    )(place, learner_gate_up, rollout_gate_up)

    def along(value, sign):
        perm = [
            (i * 2 + core, (i + sign * (1 - 2 * core)) % ring * 2 + core)
            for i in range(ring)
            for core in range(2)
        ]
        return lax.ppermute(value, ("z_hi", "core"), perm)

    first = along(synced, 1)
    second = along(synced, -1)

    synced, shared = lax.optimization_barrier((synced, shared))
    outgoing = pl.pallas_call(
        dispatch_kernel,
        out_shape=jax.ShapeDtypeStruct(
            (expert_count, PARTS, step_count * CAP, ring * BLOCK), jnp.bfloat16
        ),
        compiler_params=pltpu.CompilerParams(vmem_limit_bytes=VMEM_BYTES),
        name="dispatch_rows",
    )(shared)
    outgoing, first = lax.optimization_barrier((outgoing, first))
    far = along(first, 1)
    arrived = lax.all_to_all(outgoing, "expert", split_axis=0, concat_axis=0, tiled=True)
    arrived, second, far = lax.optimization_barrier((arrived, second, far))
    own = arrived.reshape(PARTS * slots, ring * BLOCK)
    other = lax.ppermute(own, "core", [(0, 1), (1, 0)])

    down_other = lax.ppermute(down_weight, "core", [(0, 1), (1, 0)])

    partial = pl.pallas_call(
        gate_up_kernel,
        out_shape=jax.ShapeDtypeStruct((PARTS, slots, 2 * units), jnp.bfloat16),
        compiler_params=pltpu.CompilerParams(vmem_limit_bytes=VMEM_BYTES),
        name="gate_up",
    )(own, other, synced, first, second, far)
    partial = lax.all_to_all(partial, ("z_lo", "x_lo"), split_axis=0, concat_axis=0, tiled=True)
    both = jnp.sum(partial.astype(jnp.float32), axis=0)
    hidden = (jax.nn.silu(both[:, :units]) * both[:, units:]).astype(jnp.bfloat16)
    hidden_other = lax.ppermute(hidden, "core", [(0, 1), (1, 0)])
    low = pl.BlockSpec((1, units, quarter), lambda i, p: (0, 0, p[0]))
    high = pl.BlockSpec((1, units, quarter), lambda i, p: (0, 0, 2 + p[0]))
    sides = tensor_count // 2
    expert_out = call(
        down_kernel,
        jax.ShapeDtypeStruct((sides, slots, quarter), jnp.bfloat16),
        [whole(slots, units), whole(slots, units), low, high, low, high],
        whole(sides, slots, quarter),
        "down",
    )(place, hidden, hidden_other, down_weight, down_weight, down_other, down_other)
    back = lax.all_to_all(
        expert_out.reshape(sides * expert_count, step_count * CAP, quarter),
        ("x_hi", "expert"),
        split_axis=0,
        concat_axis=0,
        tiled=True,
    )
    mixed = jnp.dot(
        jnp.concatenate([combine] * sides, axis=1),
        back.reshape(sides * slots, quarter).astype(jnp.float32),
        precision=lax.Precision.HIGHEST,
    )
    return mixed.astype(jnp.bfloat16).reshape(step_count, token_count, quarter)


def solution(mesh):
    groups, experts, tensors = mesh.devices.shape
    split = Mesh(
        mesh.devices.reshape(groups // PARTS, PARTS // 2, 2, experts, tensors // 2, 2),
        ("z_hi", "z_lo", "x_lo", "expert", "x_hi", "core"),
    )
    group, tensor = ("z_hi", "z_lo", "x_lo"), ("x_hi", "core")
    in_specs = (
        P(None, (*group, "expert"), None),
        P(None, (*group, "expert"), None),
        P(None, (*group, "expert"), None),
        P("expert", None, None, tensor),
        P("expert", None, group, tensor),
        P("expert", tensor, None),
    )
    out_specs = P(None, (*group, "expert"), tensor)
    return jax.shard_map(shards, mesh=split, in_specs=in_specs, out_specs=out_specs, check_vma=False)
```

```python
import jax
import jax.numpy as jnp
from jax import lax
from jax.experimental import pallas as pl
from jax.experimental.pallas import tpu as pltpu
from jax.sharding import Mesh
from jax.sharding import PartitionSpec as P

BLOCK = 128
CAP = 4
STEP_SLOTS = 16
PARTS = 6
VMEM_BYTES = 48 * 1024 * 1024

clip_level = 2.0
epsilon = 1e-06


def sync_kernel(place, learner, rollout, out):
    core = place[0]
    units = learner.shape[3]
    for half in range(learner.shape[2] // BLOCK):
        rows = pl.ds(pl.multiple_of((half ^ core) * BLOCK, BLOCK), BLOCK)
        for matrix in range(2):
            for column in range(units // BLOCK):
                columns = pl.ds(column * BLOCK, BLOCK)
                current = rollout[0, matrix, rows, columns].astype(jnp.float32)
                change = learner[0, matrix, rows, columns] - current
                mean_square = jnp.sum(change * change, keepdims=True) * (1.0 / (BLOCK * BLOCK))
                scale = jnp.sqrt(mean_square + epsilon).astype(jnp.bfloat16).astype(jnp.float32)
                levels = jnp.clip(change / scale, -clip_level, clip_level)
                levels = levels.astype(jnp.bfloat16).astype(jnp.float32)
                out[half, :, pl.ds(matrix * units + column * BLOCK, BLOCK)] = (
                    current + levels * scale
                ).astype(jnp.bfloat16)


def slot_choice(first, second, experts, steps):
    rows = first.shape[0]
    per_step = rows // steps
    slots = experts * steps * CAP
    row = lax.broadcasted_iota(jnp.int32, (rows, slots), 0)
    slot = lax.broadcasted_iota(jnp.int32, (rows, slots), 1)
    expert = (slot // (steps * CAP)).astype(jnp.float32)
    from_first, from_second = first == expert, second == expert
    named = (from_first | from_second).astype(jnp.float32)
    later = lax.broadcasted_iota(jnp.int32, (rows, rows), 0)
    earlier = lax.broadcasted_iota(jnp.int32, (rows, rows), 1)
    before = (earlier < later) & (earlier // per_step == later // per_step)
    rank = jnp.dot(
        before.astype(jnp.bfloat16), named.astype(jnp.bfloat16), preferred_element_type=jnp.float32
    )
    here = (slot // CAP % steps == row // per_step) & (rank == (slot % CAP).astype(jnp.float32))
    return from_first & here, from_second & here


def pack_kernel(place, ids, gates, tokens, outgoing, combine):
    core, z_high = place[0], place[3]
    owners = (z_high, z_high ^ (1 + 2 * core), z_high ^ (3 - 2 * core), z_high ^ 2)
    parts, rows, columns = outgoing.shape
    pieces = columns // BLOCK - 1
    steps = rows // 8
    experts = combine.shape[1] // (steps * CAP)
    first, second = ids[:, 0:1].astype(jnp.float32), ids[:, 1:2].astype(jnp.float32)
    chosen_first, chosen_second = slot_choice(first, second, experts, steps)
    combine[...] = jnp.where(chosen_first, gates[:, 0:1], 0.0) + jnp.where(
        chosen_second, gates[:, 1:2], 0.0
    )
    lane = lax.broadcasted_iota(jnp.int32, (rows, BLOCK), 1)
    tail = jnp.where(lane == 0, first, jnp.where(lane == 1, second, 0.0)).astype(jnp.bfloat16)
    for part in range(parts):
        for piece in range(pieces):
            start = ((owners[piece] * parts + part) * 2 + core) * BLOCK
            outgoing[part, :, piece * BLOCK : (piece + 1) * BLOCK] = tokens[
                :, pl.ds(pl.multiple_of(start, BLOCK), BLOCK)
            ]
        outgoing[part, :, pieces * BLOCK :] = tail


def dispatch_kernel(arrived, outgoing):
    experts, parts, step_slots, columns = outgoing.shape
    steps = step_slots // CAP
    for part in range(parts):
        tail = arrived[part, :, columns:].astype(jnp.float32)
        chosen_first, chosen_second = slot_choice(tail[:, 0:1], tail[:, 1:2], experts, steps)
        select = (chosen_first | chosen_second).astype(jnp.float32).astype(jnp.bfloat16)
        moved = lax.dot_general(
            select,
            arrived[part, :, :columns],
            (((0,), (0,)), ((), ())),
            preferred_element_type=jnp.float32,
        ).astype(jnp.bfloat16)
        for expert in range(experts):
            outgoing[expert, part] = moved[expert * step_slots : (expert + 1) * step_slots]


def gate_up_kernel(own, other, here, first, second, far, out):
    total = None
    for piece, (across, weights) in enumerate(((0, here), (2, first), (1, second), (3, far))):
        rows = jnp.concatenate(
            [
                own[:, piece * BLOCK : (piece + 1) * BLOCK],
                other[:, across * BLOCK : (across + 1) * BLOCK],
            ],
            axis=1,
        )
        term = jnp.dot(
            rows,
            weights[...].reshape(2 * BLOCK, weights.shape[2]),
            preferred_element_type=jnp.float32,
        )
        total = term if total is None else total + term
    partial = total.astype(jnp.bfloat16)
    parts, slots, _ = out.shape
    experts = own.shape[0] // (parts * STEP_SLOTS)
    for expert in range(experts):
        for part in range(parts):
            at = (expert * parts + part) * STEP_SLOTS
            out[part, expert * STEP_SLOTS : (expert + 1) * STEP_SLOTS] = partial[
                at : at + STEP_SLOTS
            ]


def down_kernel(place, hidden, own, crossed, sibling, out):
    units = own.shape[1]
    tensor = place[1]
    total = None
    for flip, columns in enumerate((own[0], sibling[0], crossed[...], sibling[1])):
        at = pl.ds(pl.multiple_of((tensor ^ flip) * units, units), units)
        term = jnp.dot(hidden[:, at], columns, preferred_element_type=jnp.float32)
        total = term if total is None else total + term
    out[...] = total.astype(jnp.bfloat16)


def shards(tokens, expert_ids, gate_values, rollout_gate_up, learner_gate_up, down_weight):
    ring = lax.axis_size("z_hi")
    expert_count = lax.axis_size("expert")
    tensor_count = lax.axis_size(("x_hi", "core"))
    step_count, token_count, width = tokens.shape
    quarter = width // tensor_count
    own_rows, units = learner_gate_up.shape[2:]
    slots = expert_count * step_count * CAP
    tensor = lax.axis_index(("x_hi", "core"))
    group = lax.axis_index(("z_hi", "z_lo", "x_lo"))
    place = jnp.stack([tensor % 2, tensor, group, group // PARTS]).astype(jnp.int32)

    def whole(*shape):
        return pl.BlockSpec(shape, lambda i, p: (0,) * len(shape))

    def call(body, out_shape, in_specs, out_specs, name):
        return pl.pallas_call(
            body,
            grid_spec=pltpu.PrefetchScalarGridSpec(
                num_scalar_prefetch=1, grid=(1,), in_specs=in_specs, out_specs=out_specs
            ),
            out_shape=out_shape,
            compiler_params=pltpu.CompilerParams(vmem_limit_bytes=VMEM_BYTES),
            name=name,
        )

    flat_tokens = tokens.reshape(step_count * token_count, width)
    rows = step_count * token_count
    packed, combine = call(
        pack_kernel,
        [
            jax.ShapeDtypeStruct((PARTS, rows, (ring + 1) * BLOCK), jnp.bfloat16),
            jax.ShapeDtypeStruct((rows, slots), jnp.float32),
        ],
        [whole(rows, 2), whole(rows, 2), whole(rows, width)],
        [whole(PARTS, rows, (ring + 1) * BLOCK), whole(rows, slots)],
        "pack_rows",
    )(place, expert_ids.reshape(rows, 2), gate_values.reshape(rows, 2), flat_tokens)
    shared = lax.all_to_all(packed, ("z_lo", "x_lo"), split_axis=0, concat_axis=0, tiled=True)

    packed, learner_gate_up = lax.optimization_barrier((packed, learner_gate_up))
    synced = call(
        sync_kernel,
        jax.ShapeDtypeStruct((2, own_rows // 2, 2 * units), jnp.bfloat16),
        [
            whole(1, 2, own_rows, units),
            pl.BlockSpec((1, 2, own_rows, units), lambda i, p: (0, 0, p[2], 0)),
        ],
        whole(2, own_rows // 2, 2 * units),
        "sync_rows",
    )(place, learner_gate_up, rollout_gate_up)

    def paired(value, turn):
        perm = [
            (i * 2 + core, (i ^ (1 if core == turn else 3)) * 2 + core)
            for i in range(ring)
            for core in range(2)
        ]
        return lax.ppermute(value, ("z_hi", "core"), perm)

    first = paired(synced, 0)
    second = paired(synced, 1)

    synced, shared = lax.optimization_barrier((synced, shared))
    outgoing = pl.pallas_call(
        dispatch_kernel,
        out_shape=jax.ShapeDtypeStruct(
            (expert_count, PARTS, step_count * CAP, ring * BLOCK), jnp.bfloat16
        ),
        compiler_params=pltpu.CompilerParams(vmem_limit_bytes=VMEM_BYTES),
        name="dispatch_rows",
    )(shared)
    outgoing, first = lax.optimization_barrier((outgoing, first))
    second, down_later = lax.optimization_barrier((second, down_weight))
    far = paired(first, 1)
    arrived = lax.all_to_all(outgoing, "expert", split_axis=0, concat_axis=0, tiled=True)
    arrived, second, far = lax.optimization_barrier((arrived, second, far))
    own = arrived.reshape(PARTS * slots, ring * BLOCK)
    other = lax.ppermute(own, "core", [(0, 1), (1, 0)])

    crossed = lax.ppermute(
        lax.dynamic_slice_in_dim(down_later[0], (1 - tensor // 2) * 2 * quarter, 2 * quarter, 1),
        ("x_lo", "x_hi", "core"),
        [(i, i ^ 6) for i in range(8)],
    )
    sibling = lax.ppermute(
        jnp.stack(
            [
                lax.dynamic_slice_in_dim(down_weight[0], (tensor ^ 1) * quarter, quarter, 1),
                lax.dynamic_slice_in_dim(crossed, (1 - tensor % 2) * quarter, quarter, 1),
            ]
        ),
        "core",
        [(0, 1), (1, 0)],
    )

    partial = pl.pallas_call(
        gate_up_kernel,
        out_shape=jax.ShapeDtypeStruct((PARTS, slots, 2 * units), jnp.bfloat16),
        compiler_params=pltpu.CompilerParams(vmem_limit_bytes=VMEM_BYTES),
        name="gate_up",
    )(own, other, synced, first, second, far)
    partial = lax.all_to_all(partial, ("z_lo", "x_lo"), split_axis=0, concat_axis=0, tiled=True)
    both = jnp.sum(partial.astype(jnp.float32), axis=0)
    hidden = (jax.nn.silu(both[:, :units]) * both[:, units:]).astype(jnp.bfloat16)
    hidden = lax.all_gather(hidden, ("x_hi", "core"), axis=1, tiled=True)
    expert_out = call(
        down_kernel,
        jax.ShapeDtypeStruct((slots, quarter), jnp.bfloat16),
        [
            whole(slots, tensor_count * units),
            pl.BlockSpec((1, units, quarter), lambda i, p: (0, 0, p[1])),
            pl.BlockSpec((units, quarter), lambda i, p: (0, p[0])),
            whole(2, units, quarter),
        ],
        whole(slots, quarter),
        "down",
    )(place, hidden, down_weight, crossed, sibling)
    back = lax.all_to_all(
        expert_out.reshape(expert_count, step_count * CAP, quarter),
        "expert",
        split_axis=0,
        concat_axis=0,
        tiled=True,
    )
    mixed = jnp.dot(
        combine,
        back.reshape(slots, quarter).astype(jnp.float32),
        precision=lax.Precision.HIGHEST,
    )
    return mixed.astype(jnp.bfloat16).reshape(step_count, token_count, quarter)


def solution(mesh):
    groups, experts, tensors = mesh.devices.shape
    split = Mesh(
        mesh.devices.reshape(groups // PARTS, PARTS // 2, 2, experts, tensors // 2, 2),
        ("z_hi", "z_lo", "x_lo", "expert", "x_hi", "core"),
    )
    group, tensor = ("z_hi", "z_lo", "x_lo"), ("x_hi", "core")
    in_specs = (
        P(None, (*group, "expert"), None),
        P(None, (*group, "expert"), None),
        P(None, (*group, "expert"), None),
        P("expert", None, None, tensor),
        P("expert", None, group, tensor),
        P("expert", tensor, None),
    )
    out_specs = P(None, (*group, "expert"), tensor)
    return jax.shard_map(shards, mesh=split, in_specs=in_specs, out_specs=out_specs, check_vma=False)
```

```python
import jax
import jax.numpy as jnp
from jax import lax
from jax.experimental import pallas as pl
from jax.experimental.pallas import tpu as pltpu
from jax.sharding import Mesh
from jax.sharding import PartitionSpec as P

BLOCK = 128
CAP = 4
PARTS = 6
ORDER = (0, -1, 1, 2)
VMEM_BYTES = 48 * 1024 * 1024

clip_level = 2.0
epsilon = 1e-06


def sync_kernel(place, learner, rollout, out):
    core = place[0]
    units = learner.shape[3]
    for half in range(learner.shape[2] // BLOCK):
        rows = pl.ds(pl.multiple_of((half ^ core) * BLOCK, BLOCK), BLOCK)
        for matrix in range(2):
            for column in range(units // BLOCK):
                columns = pl.ds(column * BLOCK, BLOCK)
                current = rollout[0, matrix, rows, columns].astype(jnp.float32)
                change = learner[0, matrix, rows, columns] - current
                mean_square = jnp.sum(change * change, keepdims=True) * (1.0 / (BLOCK * BLOCK))
                scale = jnp.sqrt(mean_square + epsilon).astype(jnp.bfloat16).astype(jnp.float32)
                levels = jnp.clip(change / scale, -clip_level, clip_level)
                levels = levels.astype(jnp.bfloat16).astype(jnp.float32)
                out[half, :, pl.ds(matrix * units + column * BLOCK, BLOCK)] = (
                    current + levels * scale
                ).astype(jnp.bfloat16)


def dispatch_kernel(place, ids_row, ids_col, gates_col, tokens, outgoing, combine):
    core, z_high = place[0], place[3]
    sign = 1 - 2 * core
    pieces = outgoing.shape[3] // BLOCK
    experts, step_slots = outgoing.shape[1:3]
    count = ids_row.shape[1]
    rows = count // 2
    steps = step_slots // CAP
    per_step = rows // steps
    slots = experts * step_slots
    i_row = lax.broadcasted_iota(jnp.int32, (count, count), 1)
    i_col = lax.broadcasted_iota(jnp.int32, (count, count), 0)
    same_step = (i_row % rows) // per_step == (i_col % rows) // per_step
    same = (ids_row[...] == ids_col[...]) & same_step
    rank_row = jnp.sum((same & (i_col < i_row)).astype(jnp.float32), axis=0, keepdims=True)
    rank_col = jnp.sum((same & (i_row < i_col)).astype(jnp.float32), axis=1, keepdims=True)
    step_row = (lax.broadcasted_iota(jnp.int32, (1, count), 1) % rows) // per_step
    step_col = (lax.broadcasted_iota(jnp.int32, (count, 1), 0) % rows) // per_step
    slot_row = ids_row[...] * step_slots + step_row * CAP + rank_row.astype(jnp.int32)
    slot_col = ids_col[...] * step_slots + step_col * CAP + rank_col.astype(jnp.int32)
    matches = lax.broadcasted_iota(jnp.int32, (slots, count), 0) == slot_row
    hot = matches.astype(jnp.float32)
    select = (hot[:, :rows] + hot[:, rows:]).astype(jnp.bfloat16)
    weighted = jnp.where(
        lax.broadcasted_iota(jnp.int32, (count, slots), 1) == slot_col, gates_col[...], 0.0
    )
    combine[...] = weighted[:rows] + weighted[rows:]
    for part in range(PARTS):
        for piece in range(pieces):
            owner = lax.rem(z_high + sign * ORDER[piece] + pieces, pieces)
            start = ((owner * PARTS + part) * 2 + core) * BLOCK
            columns = tokens[:, pl.ds(pl.multiple_of(start, BLOCK), BLOCK)]
            moved = jnp.dot(select, columns, preferred_element_type=jnp.float32)
            outgoing[part, :, :, piece * BLOCK : (piece + 1) * BLOCK] = moved.astype(
                jnp.bfloat16
            ).reshape(experts, step_slots, BLOCK)


def gate_up_kernel(own, other, here, first, second, far, out):
    total = None
    for piece, (across, weights) in enumerate(((0, here), (2, first), (1, second), (3, far))):
        rows = jnp.concatenate(
            [
                own[:, piece * BLOCK : (piece + 1) * BLOCK],
                other[:, across * BLOCK : (across + 1) * BLOCK],
            ],
            axis=1,
        )
        term = jnp.dot(
            rows,
            weights[...].reshape(2 * BLOCK, weights.shape[2]),
            preferred_element_type=jnp.float32,
        )
        total = term if total is None else total + term
    out[...] = total.astype(jnp.bfloat16)


def down_kernel(place, hidden, own, crossed, sibling, out):
    units = own.shape[1]
    tensor = place[1]
    total = None
    for flip, columns in enumerate((own[0], sibling[0], crossed[...], sibling[1])):
        at = pl.ds(pl.multiple_of((tensor ^ flip) * units, units), units)
        term = jnp.dot(hidden[:, at], columns, preferred_element_type=jnp.float32)
        total = term if total is None else total + term
    out[...] = total.astype(jnp.bfloat16)


def shards(tokens, expert_ids, gate_values, rollout_gate_up, learner_gate_up, down_weight):
    ring = lax.axis_size("z_hi")
    expert_count = lax.axis_size("expert")
    tensor_count = lax.axis_size(("x_hi", "core"))
    step_count, token_count, width = tokens.shape
    quarter = width // tensor_count
    own_rows, units = learner_gate_up.shape[2:]
    slots = expert_count * step_count * CAP
    tensor = lax.axis_index(("x_hi", "core"))
    group = lax.axis_index(("z_hi", "z_lo", "x_lo"))
    place = jnp.stack([tensor % 2, tensor, group, group // PARTS]).astype(jnp.int32)

    def whole(*shape):
        return pl.BlockSpec(shape, lambda i, p: (0,) * len(shape))

    def call(body, out_shape, in_specs, out_specs, name):
        return pl.pallas_call(
            body,
            grid_spec=pltpu.PrefetchScalarGridSpec(
                num_scalar_prefetch=1, grid=(1,), in_specs=in_specs, out_specs=out_specs
            ),
            out_shape=out_shape,
            compiler_params=pltpu.CompilerParams(vmem_limit_bytes=VMEM_BYTES),
            name=name,
        )

    synced = call(
        sync_kernel,
        jax.ShapeDtypeStruct((2, own_rows // 2, 2 * units), jnp.bfloat16),
        [
            whole(1, 2, own_rows, units),
            pl.BlockSpec((1, 2, own_rows, units), lambda i, p: (0, 0, p[2], 0)),
        ],
        whole(2, own_rows // 2, 2 * units),
        "sync_rows",
    )(place, learner_gate_up, rollout_gate_up)

    def along(value, sign):
        perm = [
            (i * 2 + core, (i + sign * (1 - 2 * core)) % ring * 2 + core)
            for i in range(ring)
            for core in range(2)
        ]
        return lax.ppermute(value, ("z_hi", "core"), perm)

    first = along(synced, 1)
    second = along(synced, -1)

    synced, expert_ids = lax.optimization_barrier((synced, expert_ids))
    flat_ids = expert_ids.transpose(2, 0, 1).reshape(-1)
    flat_gates = gate_values.transpose(2, 0, 1).reshape(-1)
    flat_tokens = tokens.reshape(step_count * token_count, width)
    count = flat_ids.shape[0]
    out_dims = (PARTS, expert_count, step_count * CAP, ring * BLOCK)
    outgoing, combine = call(
        dispatch_kernel,
        [
            jax.ShapeDtypeStruct(out_dims, jnp.bfloat16),
            jax.ShapeDtypeStruct((count // 2, slots), jnp.float32),
        ],
        [whole(1, count), whole(count, 1), whole(count, 1), whole(*flat_tokens.shape)],
        [whole(*out_dims), whole(count // 2, slots)],
        "dispatch_rows",
    )(
        place,
        flat_ids.reshape(1, count),
        flat_ids.reshape(count, 1),
        flat_gates.reshape(count, 1),
        flat_tokens,
    )
    down_half = lax.dynamic_slice_in_dim(
        down_weight[0], (1 - tensor // 2) * 2 * quarter, 2 * quarter, 1
    )
    outgoing, first, down_half = lax.optimization_barrier((outgoing, first, down_half))
    far = along(first, 1)
    arrived = lax.all_to_all(
        outgoing.reshape(PARTS * expert_count, step_count * CAP, ring * BLOCK),
        ("z_lo", "x_lo", "expert"),
        split_axis=0,
        concat_axis=0,
        tiled=True,
    )
    arrived, second, far = lax.optimization_barrier((arrived, second, far))
    own = arrived.reshape(PARTS * slots, ring * BLOCK)
    other = lax.ppermute(own, "core", [(0, 1), (1, 0)])

    crossed = lax.ppermute(
        down_half,
        ("x_lo", "x_hi", "core"),
        [(i, i ^ 6) for i in range(8)],
    )
    sibling = lax.ppermute(
        jnp.stack(
            [
                lax.dynamic_slice_in_dim(down_weight[0], (tensor ^ 1) * quarter, quarter, 1),
                lax.dynamic_slice_in_dim(crossed, (1 - tensor % 2) * quarter, quarter, 1),
            ]
        ),
        "core",
        [(0, 1), (1, 0)],
    )

    partial = pl.pallas_call(
        gate_up_kernel,
        out_shape=jax.ShapeDtypeStruct((PARTS * slots, 2 * units), jnp.bfloat16),
        compiler_params=pltpu.CompilerParams(vmem_limit_bytes=VMEM_BYTES),
        name="gate_up",
    )(own, other, synced, first, second, far)
    partial = lax.all_to_all(
        partial.reshape(PARTS, slots, 2 * units),
        ("z_lo", "x_lo"),
        split_axis=0,
        concat_axis=0,
        tiled=True,
    )
    both = jnp.sum(partial.astype(jnp.float32), axis=0)
    hidden = (jax.nn.silu(both[:, :units]) * both[:, units:]).astype(jnp.bfloat16)
    hidden = lax.all_gather(hidden, ("x_hi", "core"), axis=1, tiled=True)
    expert_out = call(
        down_kernel,
        jax.ShapeDtypeStruct((slots, quarter), jnp.bfloat16),
        [
            whole(slots, tensor_count * units),
            pl.BlockSpec((1, units, quarter), lambda i, p: (0, 0, p[1])),
            pl.BlockSpec((units, quarter), lambda i, p: (0, p[0])),
            whole(2, units, quarter),
        ],
        whole(slots, quarter),
        "down",
    )(place, hidden, down_weight, crossed, sibling)
    back = lax.all_to_all(
        expert_out.reshape(expert_count, step_count * CAP, quarter),
        "expert",
        split_axis=0,
        concat_axis=0,
        tiled=True,
    )
    mixed = jnp.dot(
        combine,
        back.reshape(slots, quarter).astype(jnp.float32),
        precision=lax.Precision.HIGHEST,
    )
    return mixed.astype(jnp.bfloat16).reshape(step_count, token_count, quarter)


def solution(mesh):
    groups, experts, tensors = mesh.devices.shape
    split = Mesh(
        mesh.devices.reshape(groups // PARTS, PARTS // 2, 2, experts, tensors // 2, 2),
        ("z_hi", "z_lo", "x_lo", "expert", "x_hi", "core"),
    )
    group, tensor = ("z_hi", "z_lo", "x_lo"), ("x_hi", "core")
    in_specs = (
        P(None, (*group, "expert"), None),
        P(None, (*group, "expert"), None),
        P(None, (*group, "expert"), None),
        P("expert", None, None, tensor),
        P("expert", None, group, tensor),
        P("expert", tensor, None),
    )
    out_specs = P(None, (*group, "expert"), tensor)
    return jax.shard_map(shards, mesh=split, in_specs=in_specs, out_specs=out_specs, check_vma=False)
```

```python
import jax
import jax.numpy as jnp
from jax import lax
from jax.experimental import pallas as pl
from jax.experimental.pallas import tpu as pltpu
from jax.sharding import Mesh
from jax.sharding import PartitionSpec as P

BLOCK = 128
CAP = 4
PARTS = 6
ORDER = (0, -1, 1, 2)
VMEM_BYTES = 48 * 1024 * 1024

clip_level = 2.0
epsilon = 1e-06


def sync_kernel(place, learner, rollout, out):
    core = place[0]
    units = learner.shape[3]
    for half in range(learner.shape[2] // BLOCK):
        rows = pl.ds(pl.multiple_of((half ^ core) * BLOCK, BLOCK), BLOCK)
        for matrix in range(2):
            for column in range(units // BLOCK):
                columns = pl.ds(column * BLOCK, BLOCK)
                current = rollout[0, matrix, rows, columns].astype(jnp.float32)
                change = learner[0, matrix, rows, columns] - current
                mean_square = jnp.sum(change * change, keepdims=True) * (1.0 / (BLOCK * BLOCK))
                scale = jnp.sqrt(mean_square + epsilon).astype(jnp.bfloat16).astype(jnp.float32)
                levels = jnp.clip(change / scale, -clip_level, clip_level)
                levels = levels.astype(jnp.bfloat16).astype(jnp.float32)
                out[half, :, pl.ds(matrix * units + column * BLOCK, BLOCK)] = (
                    current + levels * scale
                ).astype(jnp.bfloat16)


def dispatch_kernel(place, ids_row, ids_col, gates_col, tokens, outgoing, combine):
    core, z_high = place[0], place[3]
    sign = 1 - 2 * core
    pieces = outgoing.shape[3] // BLOCK
    experts, step_slots = outgoing.shape[1:3]
    count = ids_row.shape[1]
    rows = count // 2
    steps = step_slots // CAP
    per_step = rows // steps
    slots = experts * step_slots
    i_row = lax.broadcasted_iota(jnp.int32, (count, count), 1)
    i_col = lax.broadcasted_iota(jnp.int32, (count, count), 0)
    same_step = (i_row % rows) // per_step == (i_col % rows) // per_step
    same = (ids_row[...] == ids_col[...]) & same_step
    rank_row = jnp.sum((same & (i_col < i_row)).astype(jnp.float32), axis=0, keepdims=True)
    rank_col = jnp.sum((same & (i_row < i_col)).astype(jnp.float32), axis=1, keepdims=True)
    step_row = (lax.broadcasted_iota(jnp.int32, (1, count), 1) % rows) // per_step
    step_col = (lax.broadcasted_iota(jnp.int32, (count, 1), 0) % rows) // per_step
    slot_row = ids_row[...] * step_slots + step_row * CAP + rank_row.astype(jnp.int32)
    slot_col = ids_col[...] * step_slots + step_col * CAP + rank_col.astype(jnp.int32)
    matches = lax.broadcasted_iota(jnp.int32, (slots, count), 0) == slot_row
    hot = matches.astype(jnp.float32)
    select = (hot[:, :rows] + hot[:, rows:]).astype(jnp.bfloat16)
    weighted = jnp.where(
        lax.broadcasted_iota(jnp.int32, (count, slots), 1) == slot_col, gates_col[...], 0.0
    )
    combine[...] = weighted[:rows] + weighted[rows:]
    for part in range(PARTS):
        for piece in range(pieces):
            owner = lax.rem(z_high + sign * ORDER[piece] + pieces, pieces)
            start = ((owner * PARTS + part) * 2 + core) * BLOCK
            columns = tokens[:, pl.ds(pl.multiple_of(start, BLOCK), BLOCK)]
            moved = jnp.dot(select, columns, preferred_element_type=jnp.float32)
            outgoing[part, :, :, piece * BLOCK : (piece + 1) * BLOCK] = moved.astype(
                jnp.bfloat16
            ).reshape(experts, step_slots, BLOCK)


def gate_up_kernel(own, other, here, first, second, far, out):
    total = None
    for piece, (across, weights) in enumerate(((0, here), (2, first), (1, second), (3, far))):
        rows = jnp.concatenate(
            [
                own[:, piece * BLOCK : (piece + 1) * BLOCK],
                other[:, across * BLOCK : (across + 1) * BLOCK],
            ],
            axis=1,
        )
        term = jnp.dot(
            rows,
            weights[...].reshape(2 * BLOCK, weights.shape[2]),
            preferred_element_type=jnp.float32,
        )
        total = term if total is None else total + term
    out[...] = total.astype(jnp.bfloat16)


def down_kernel(place, hidden, own, crossed, sibling, out):
    units = own.shape[1]
    tensor = place[1]
    total = None
    for flip, columns in enumerate((own[0], sibling[0], crossed[...], sibling[1])):
        at = pl.ds(pl.multiple_of((tensor ^ flip) * units, units), units)
        term = jnp.dot(hidden[:, at], columns, preferred_element_type=jnp.float32)
        total = term if total is None else total + term
    out[...] = total.astype(jnp.bfloat16)


def shards(tokens, expert_ids, gate_values, rollout_gate_up, learner_gate_up, down_weight):
    ring = lax.axis_size("z_hi")
    expert_count = lax.axis_size("expert")
    tensor_count = lax.axis_size(("x_hi", "core"))
    step_count, token_count, width = tokens.shape
    quarter = width // tensor_count
    own_rows, units = learner_gate_up.shape[2:]
    slots = expert_count * step_count * CAP
    tensor = lax.axis_index(("x_hi", "core"))
    group = lax.axis_index(("z_hi", "z_lo", "x_lo"))
    place = jnp.stack([tensor % 2, tensor, group, group // PARTS]).astype(jnp.int32)

    def whole(*shape):
        return pl.BlockSpec(shape, lambda i, p: (0,) * len(shape))

    def call(body, out_shape, in_specs, out_specs, name):
        return pl.pallas_call(
            body,
            grid_spec=pltpu.PrefetchScalarGridSpec(
                num_scalar_prefetch=1, grid=(1,), in_specs=in_specs, out_specs=out_specs
            ),
            out_shape=out_shape,
            compiler_params=pltpu.CompilerParams(vmem_limit_bytes=VMEM_BYTES),
            name=name,
        )

    synced = call(
        sync_kernel,
        jax.ShapeDtypeStruct((2, own_rows // 2, 2 * units), jnp.bfloat16),
        [
            whole(1, 2, own_rows, units),
            pl.BlockSpec((1, 2, own_rows, units), lambda i, p: (0, 0, p[2], 0)),
        ],
        whole(2, own_rows // 2, 2 * units),
        "sync_rows",
    )(place, learner_gate_up, rollout_gate_up)

    def along(value, sign):
        perm = [
            (i * 2 + core, (i + sign * (1 - 2 * core)) % ring * 2 + core)
            for i in range(ring)
            for core in range(2)
        ]
        return lax.ppermute(value, ("z_hi", "core"), perm)

    first = along(synced, 1)
    second = along(synced, -1)

    synced, expert_ids = lax.optimization_barrier((synced, expert_ids))
    flat_ids = expert_ids.transpose(2, 0, 1).reshape(-1)
    flat_gates = gate_values.transpose(2, 0, 1).reshape(-1)
    flat_tokens = tokens.reshape(step_count * token_count, width)
    count = flat_ids.shape[0]
    out_dims = (PARTS, expert_count, step_count * CAP, ring * BLOCK)
    outgoing, combine = call(
        dispatch_kernel,
        [
            jax.ShapeDtypeStruct(out_dims, jnp.bfloat16),
            jax.ShapeDtypeStruct((count // 2, slots), jnp.float32),
        ],
        [whole(1, count), whole(count, 1), whole(count, 1), whole(*flat_tokens.shape)],
        [whole(*out_dims), whole(count // 2, slots)],
        "dispatch_rows",
    )(
        place,
        flat_ids.reshape(1, count),
        flat_ids.reshape(count, 1),
        flat_gates.reshape(count, 1),
        flat_tokens,
    )
    down_half = lax.dynamic_slice_in_dim(
        down_weight[0], (1 - tensor // 2) * 2 * quarter, 2 * quarter, 1
    )
    outgoing, first, second, down_half = lax.optimization_barrier(
        (outgoing, first, second, down_half)
    )
    far = along(first, 1)
    arrived = lax.all_to_all(
        outgoing.reshape(PARTS * expert_count, step_count * CAP, ring * BLOCK),
        ("z_lo", "x_lo", "expert"),
        split_axis=0,
        concat_axis=0,
        tiled=True,
    )
    arrived, far = lax.optimization_barrier((arrived, far))
    own = arrived.reshape(PARTS * slots, ring * BLOCK)
    other = lax.ppermute(own, "core", [(0, 1), (1, 0)])

    crossed = lax.ppermute(
        down_half,
        ("x_lo", "x_hi", "core"),
        [(i, i ^ 6) for i in range(8)],
    )
    sibling = lax.ppermute(
        jnp.stack(
            [
                lax.dynamic_slice_in_dim(down_weight[0], (tensor ^ 1) * quarter, quarter, 1),
                lax.dynamic_slice_in_dim(crossed, (1 - tensor % 2) * quarter, quarter, 1),
            ]
        ),
        "core",
        [(0, 1), (1, 0)],
    )

    partial = pl.pallas_call(
        gate_up_kernel,
        out_shape=jax.ShapeDtypeStruct((PARTS * slots, 2 * units), jnp.bfloat16),
        compiler_params=pltpu.CompilerParams(vmem_limit_bytes=VMEM_BYTES),
        name="gate_up",
    )(own, other, synced, first, second, far)
    partial = lax.all_to_all(
        partial.reshape(PARTS, slots, 2 * units),
        ("z_lo", "x_lo"),
        split_axis=0,
        concat_axis=0,
        tiled=True,
    )
    both = jnp.sum(partial.astype(jnp.float32), axis=0)
    hidden = (jax.nn.silu(both[:, :units]) * both[:, units:]).astype(jnp.bfloat16)
    hidden = lax.all_gather(hidden, ("x_hi", "core"), axis=1, tiled=True)
    expert_out = call(
        down_kernel,
        jax.ShapeDtypeStruct((slots, quarter), jnp.bfloat16),
        [
            whole(slots, tensor_count * units),
            pl.BlockSpec((1, units, quarter), lambda i, p: (0, 0, p[1])),
            pl.BlockSpec((units, quarter), lambda i, p: (0, p[0])),
            whole(2, units, quarter),
        ],
        whole(slots, quarter),
        "down",
    )(place, hidden, down_weight, crossed, sibling)
    back = lax.all_to_all(
        expert_out.reshape(expert_count, step_count * CAP, quarter),
        "expert",
        split_axis=0,
        concat_axis=0,
        tiled=True,
    )
    mixed = jnp.dot(
        combine,
        back.reshape(slots, quarter).astype(jnp.float32),
        precision=lax.Precision.HIGHEST,
    )
    return mixed.astype(jnp.bfloat16).reshape(step_count, token_count, quarter)


def solution(mesh):
    groups, experts, tensors = mesh.devices.shape
    split = Mesh(
        mesh.devices.reshape(groups // PARTS, PARTS // 2, 2, experts, tensors // 2, 2),
        ("z_hi", "z_lo", "x_lo", "expert", "x_hi", "core"),
    )
    group, tensor = ("z_hi", "z_lo", "x_lo"), ("x_hi", "core")
    in_specs = (
        P(None, (*group, "expert"), None),
        P(None, (*group, "expert"), None),
        P(None, (*group, "expert"), None),
        P("expert", None, None, tensor),
        P("expert", None, group, tensor),
        P("expert", tensor, None),
    )
    out_specs = P(None, (*group, "expert"), tensor)
    return jax.shard_map(shards, mesh=split, in_specs=in_specs, out_specs=out_specs, check_vma=False)
```

```python
import jax
import jax.numpy as jnp
from jax import lax
from jax.experimental import pallas as pl
from jax.experimental.pallas import tpu as pltpu
from jax.sharding import Mesh
from jax.sharding import PartitionSpec as P

BLOCK = 128
CAP = 4
PARTS = 6
ORDER = (0, -1, 1, 2)
VMEM_BYTES = 48 * 1024 * 1024

clip_level = 2.0
epsilon = 1e-06


def sync_kernel(place, learner, rollout, out):
    core = place[0]
    units = learner.shape[3]
    for half in range(learner.shape[2] // BLOCK):
        rows = pl.ds(pl.multiple_of((half ^ core) * BLOCK, BLOCK), BLOCK)
        for matrix in range(2):
            for column in range(units // BLOCK):
                columns = pl.ds(column * BLOCK, BLOCK)
                current = rollout[0, matrix, rows, columns].astype(jnp.float32)
                change = learner[0, matrix, rows, columns] - current
                mean_square = jnp.sum(change * change, keepdims=True) * (1.0 / (BLOCK * BLOCK))
                scale = jnp.sqrt(mean_square + epsilon).astype(jnp.bfloat16).astype(jnp.float32)
                levels = jnp.clip(change / scale, -clip_level, clip_level)
                levels = levels.astype(jnp.bfloat16).astype(jnp.float32)
                out[half, :, pl.ds(matrix * units + column * BLOCK, BLOCK)] = (
                    current + levels * scale
                ).astype(jnp.bfloat16)


def dispatch_kernel(place, ids_row, ids_col, gates_col, tokens, outgoing, combine):
    core, z_high = place[0], place[3]
    sign = 1 - 2 * core
    pieces = outgoing.shape[3] // BLOCK
    experts, step_slots = outgoing.shape[1:3]
    count = ids_row.shape[1]
    rows = count // 2
    steps = step_slots // CAP
    per_step = rows // steps
    slots = experts * step_slots
    i_row = lax.broadcasted_iota(jnp.int32, (count, count), 1)
    i_col = lax.broadcasted_iota(jnp.int32, (count, count), 0)
    same_step = (i_row % rows) // per_step == (i_col % rows) // per_step
    same = (ids_row[...] == ids_col[...]) & same_step
    rank_row = jnp.sum((same & (i_col < i_row)).astype(jnp.float32), axis=0, keepdims=True)
    rank_col = jnp.sum((same & (i_row < i_col)).astype(jnp.float32), axis=1, keepdims=True)
    step_row = (lax.broadcasted_iota(jnp.int32, (1, count), 1) % rows) // per_step
    step_col = (lax.broadcasted_iota(jnp.int32, (count, 1), 0) % rows) // per_step
    slot_row = ids_row[...] * step_slots + step_row * CAP + rank_row.astype(jnp.int32)
    slot_col = ids_col[...] * step_slots + step_col * CAP + rank_col.astype(jnp.int32)
    matches = lax.broadcasted_iota(jnp.int32, (slots, count), 0) == slot_row
    hot = matches.astype(jnp.float32)
    select = (hot[:, :rows] + hot[:, rows:]).astype(jnp.bfloat16)
    weighted = jnp.where(
        lax.broadcasted_iota(jnp.int32, (count, slots), 1) == slot_col, gates_col[...], 0.0
    )
    combine[...] = weighted[:rows] + weighted[rows:]
    for part in range(PARTS):
        for piece in range(pieces):
            owner = lax.rem(z_high + sign * ORDER[piece] + pieces, pieces)
            start = ((owner * PARTS + part) * 2 + core) * BLOCK
            columns = tokens[:, pl.ds(pl.multiple_of(start, BLOCK), BLOCK)]
            moved = jnp.dot(select, columns, preferred_element_type=jnp.float32)
            outgoing[part, :, :, piece * BLOCK : (piece + 1) * BLOCK] = moved.astype(
                jnp.bfloat16
            ).reshape(experts, step_slots, BLOCK)


def gate_up_kernel(own, other, here, first, second, far, out):
    total = None
    for piece, (across, weights) in enumerate(((0, here), (2, first), (1, second), (3, far))):
        rows = jnp.concatenate(
            [
                own[:, piece * BLOCK : (piece + 1) * BLOCK],
                other[:, across * BLOCK : (across + 1) * BLOCK],
            ],
            axis=1,
        )
        term = jnp.dot(
            rows,
            weights[...].reshape(2 * BLOCK, weights.shape[2]),
            preferred_element_type=jnp.float32,
        )
        total = term if total is None else total + term
    out[...] = total.astype(jnp.bfloat16)


def down_kernel(place, hidden, own, crossed, sibling, out):
    units = own.shape[1]
    tensor = place[1]
    total = None
    for flip, columns in enumerate((own[0], sibling[0], crossed[...], sibling[1])):
        at = pl.ds(pl.multiple_of((tensor ^ flip) * units, units), units)
        term = jnp.dot(hidden[:, at], columns, preferred_element_type=jnp.float32)
        total = term if total is None else total + term
    out[...] = total.astype(jnp.bfloat16)


def shards(tokens, expert_ids, gate_values, rollout_gate_up, learner_gate_up, down_weight):
    ring = lax.axis_size("z_hi")
    expert_count = lax.axis_size("expert")
    tensor_count = lax.axis_size(("x_hi", "core"))
    step_count, token_count, width = tokens.shape
    quarter = width // tensor_count
    own_rows, units = learner_gate_up.shape[2:]
    slots = expert_count * step_count * CAP
    tensor = lax.axis_index(("x_hi", "core"))
    group = lax.axis_index(("z_hi", "z_lo", "x_lo"))
    place = jnp.stack([tensor % 2, tensor, group, group // PARTS]).astype(jnp.int32)

    def whole(*shape):
        return pl.BlockSpec(shape, lambda i, p: (0,) * len(shape))

    def call(body, out_shape, in_specs, out_specs, name):
        return pl.pallas_call(
            body,
            grid_spec=pltpu.PrefetchScalarGridSpec(
                num_scalar_prefetch=1, grid=(1,), in_specs=in_specs, out_specs=out_specs
            ),
            out_shape=out_shape,
            compiler_params=pltpu.CompilerParams(vmem_limit_bytes=VMEM_BYTES),
            name=name,
        )

    synced = call(
        sync_kernel,
        jax.ShapeDtypeStruct((2, own_rows // 2, 2 * units), jnp.bfloat16),
        [
            whole(1, 2, own_rows, units),
            pl.BlockSpec((1, 2, own_rows, units), lambda i, p: (0, 0, p[2], 0)),
        ],
        whole(2, own_rows // 2, 2 * units),
        "sync_rows",
    )(place, learner_gate_up, rollout_gate_up)

    def along(value, sign):
        perm = [
            (i * 2 + core, (i + sign * (1 - 2 * core)) % ring * 2 + core)
            for i in range(ring)
            for core in range(2)
        ]
        return lax.ppermute(value, ("z_hi", "core"), perm)

    first_low, first_high = along(synced[0], 1), along(synced[1], 1)
    second = along(synced, -1)

    synced, expert_ids = lax.optimization_barrier((synced, expert_ids))
    flat_ids = expert_ids.transpose(2, 0, 1).reshape(-1)
    flat_gates = gate_values.transpose(2, 0, 1).reshape(-1)
    flat_tokens = tokens.reshape(step_count * token_count, width)
    count = flat_ids.shape[0]
    out_dims = (PARTS, expert_count, step_count * CAP, ring * BLOCK)
    outgoing, combine = call(
        dispatch_kernel,
        [
            jax.ShapeDtypeStruct(out_dims, jnp.bfloat16),
            jax.ShapeDtypeStruct((count // 2, slots), jnp.float32),
        ],
        [whole(1, count), whole(count, 1), whole(count, 1), whole(*flat_tokens.shape)],
        [whole(*out_dims), whole(count // 2, slots)],
        "dispatch_rows",
    )(
        place,
        flat_ids.reshape(1, count),
        flat_ids.reshape(count, 1),
        flat_gates.reshape(count, 1),
        flat_tokens,
    )
    down_half = lax.dynamic_slice_in_dim(
        down_weight[0], (1 - tensor // 2) * 2 * quarter, 2 * quarter, 1
    )
    outgoing, first_low, down_half = lax.optimization_barrier((outgoing, first_low, down_half))
    first = jnp.stack([first_low, first_high])
    far = along(first, 1)
    arrived = lax.all_to_all(
        outgoing.reshape(PARTS * expert_count, step_count * CAP, ring * BLOCK),
        ("z_lo", "x_lo", "expert"),
        split_axis=0,
        concat_axis=0,
        tiled=True,
    )
    arrived, second, far = lax.optimization_barrier((arrived, second, far))
    own = arrived.reshape(PARTS * slots, ring * BLOCK)
    other = lax.ppermute(own, "core", [(0, 1), (1, 0)])

    crossed = lax.ppermute(
        down_half,
        ("x_lo", "x_hi", "core"),
        [(i, i ^ 6) for i in range(8)],
    )
    sibling = lax.ppermute(
        jnp.stack(
            [
                lax.dynamic_slice_in_dim(down_weight[0], (tensor ^ 1) * quarter, quarter, 1),
                lax.dynamic_slice_in_dim(crossed, (1 - tensor % 2) * quarter, quarter, 1),
            ]
        ),
        "core",
        [(0, 1), (1, 0)],
    )

    partial = pl.pallas_call(
        gate_up_kernel,
        out_shape=jax.ShapeDtypeStruct((PARTS * slots, 2 * units), jnp.bfloat16),
        compiler_params=pltpu.CompilerParams(vmem_limit_bytes=VMEM_BYTES),
        name="gate_up",
    )(own, other, synced, first, second, far)
    partial = lax.all_to_all(
        partial.reshape(PARTS, slots, 2 * units),
        ("z_lo", "x_lo"),
        split_axis=0,
        concat_axis=0,
        tiled=True,
    )
    both = jnp.sum(partial.astype(jnp.float32), axis=0)
    hidden = (jax.nn.silu(both[:, :units]) * both[:, units:]).astype(jnp.bfloat16)
    hidden = lax.all_gather(hidden, ("x_hi", "core"), axis=1, tiled=True)
    expert_out = call(
        down_kernel,
        jax.ShapeDtypeStruct((slots, quarter), jnp.bfloat16),
        [
            whole(slots, tensor_count * units),
            pl.BlockSpec((1, units, quarter), lambda i, p: (0, 0, p[1])),
            pl.BlockSpec((units, quarter), lambda i, p: (0, p[0])),
            whole(2, units, quarter),
        ],
        whole(slots, quarter),
        "down",
    )(place, hidden, down_weight, crossed, sibling)
    back = lax.all_to_all(
        expert_out.reshape(expert_count, step_count * CAP, quarter),
        "expert",
        split_axis=0,
        concat_axis=0,
        tiled=True,
    )
    mixed = jnp.dot(
        combine,
        back.reshape(slots, quarter).astype(jnp.float32),
        precision=lax.Precision.HIGHEST,
    )
    return mixed.astype(jnp.bfloat16).reshape(step_count, token_count, quarter)


def solution(mesh):
    groups, experts, tensors = mesh.devices.shape
    split = Mesh(
        mesh.devices.reshape(groups // PARTS, PARTS // 2, 2, experts, tensors // 2, 2),
        ("z_hi", "z_lo", "x_lo", "expert", "x_hi", "core"),
    )
    group, tensor = ("z_hi", "z_lo", "x_lo"), ("x_hi", "core")
    in_specs = (
        P(None, (*group, "expert"), None),
        P(None, (*group, "expert"), None),
        P(None, (*group, "expert"), None),
        P("expert", None, None, tensor),
        P("expert", None, group, tensor),
        P("expert", tensor, None),
    )
    out_specs = P(None, (*group, "expert"), tensor)
    return jax.shard_map(shards, mesh=split, in_specs=in_specs, out_specs=out_specs, check_vma=False)
```
